768 devices in a mesh: blk: 384 (over z, y, x_hi, core), inner: 2 (over x_lo).
Axes of the slice: x: 4 (x_hi: 2, x_lo: 2; x = x_hi * 2 + x_lo), y: 8, z: 12, core: 2. Of those that a mesh axis runs over, the one named last changes fastest.
Arguments:
- picture_vectors: bfloat16 [294912, 1152], P(('blk', 'inner')), may hold values from -0.29882812 to 0.29882812
- caption_vectors: bfloat16 [294912, 1152], P(('blk', 'inner')), may hold values from -0.29882812 to 0.29882812
- score_scaling: float32 [], replicated, may hold values from 5 to 20
- score_shift: float32 [], replicated, may hold values from -3 to 0
Outputs:
- loss_rows: float32 [294912], P(('blk', 'inner'))
- image_grad: bfloat16 [294912, 1152], P(('blk', 'inner'))
- text_grad: bfloat16 [294912, 1152], P(('blk', 'inner'))
The draws below stay inside these ranges and needn't reach their ends.
All inputs are finite; a program needn't handle non-finite values.
Results may differ from the reference program's by a relative error of at most 0.0061.
Values may be sent and summed in bfloat16 or wider, within the bound.
A program may use at most 32 MiB of HBM per device.

```python
import math
import jax
import jax.numpy as jnp
from jax import lax

D = 1152
ROWS_DEV = 384
SPAN = 4
PAIRS = 294912


def level_of(key, extent, shards, smallest, largest):
    def one(dim, parts):
        draws = jax.random.uniform(jax.random.fold_in(jax.random.fold_in(key, 6), dim), (parts,), jnp.float32, smallest / len(shards), largest / len(shards))
        return jnp.repeat(jnp.exp(draws), extent[dim] // parts).reshape((-1,) + (1,) * (len(extent) - dim - 1))

    gain = one(*shards[0])
    for cut in shards[1:]:
        gain = gain * one(*cut)
    return gain


def gaussian(rng, extent, scale, limit, cuts=(), held_as=jnp.bfloat16):
    drawn = scale * jax.random.normal(rng, extent, jnp.float32)
    if cuts:
        drawn = drawn * level_of(rng, extent, cuts, -0.22, 0.18)
    return jnp.clip(drawn, -limit, limit).astype(held_as)


def setup_inputs(seed: int = 0) -> dict:
    splits = jax.random.split(jax.random.key(seed), 5)
    return {
        "picture_vectors": gaussian(splits[0], (PAIRS, D), 0.05, 0.29882812, ((0, 768),)),
        "caption_vectors": gaussian(splits[1], (PAIRS, D), 0.05, 0.29882812, ((0, 768),)),
        "score_scaling": jnp.clip(jnp.exp(jax.random.uniform(splits[2], (), jnp.float32, math.log(5.0), math.log(20.0))), 5.0, 20.0),
        "score_shift": jnp.clip(jax.random.uniform(splits[3], (), jnp.float32, -3.0, 0.0), -3.0, 0.0),
    }


def normalize(block):
    values = block.astype(jnp.float32)
    length = jnp.sqrt(lax.optimization_barrier(jnp.sum(values * values, axis=-1, keepdims=True)) + 1e-06)
    return (values / length, length)

def matrix_entries(picture_summed, caption_summed, score_scaling, score_shift, first_round_indicator):
    match_scores = score_scaling * lax.dot_general(picture_summed, caption_summed, (((1,), (1,)), ((), ())), preferred_element_type=jnp.float32) + score_shift
    rows = match_scores.shape[0]
    if first_round_indicator:
        same = jnp.arange(rows)[:, None] == jnp.arange(rows)[None, :]
        match_sign = jnp.where(same, jnp.float32(1.0), jnp.float32(-1.0))
    else:
        match_sign = jnp.float32(-1.0)
    objective_total = lax.optimization_barrier(jnp.sum(jax.nn.softplus(-match_sign * match_scores), axis=1))
    score_multiplier = (-match_sign * jax.nn.sigmoid(-match_sign * match_scores) * score_scaling).astype(jnp.bfloat16)
    return (objective_total, score_multiplier)

def project(unit, grad, length):
    return (grad - unit * lax.optimization_barrier(jnp.sum(unit * grad, axis=-1, keepdims=True))) / length

def reference(picture_vectors, caption_vectors, score_scaling, score_shift):
    rows = ROWS_DEV
    count = PAIRS // rows
    image_blocks = picture_vectors.reshape(count, rows, D)
    text_blocks = caption_vectors.reshape(count, rows, D)

    def one_block(index):
        image_unit, image_length = normalize(image_blocks[index])
        text_unit, text_length = normalize(text_blocks[index])
        picture_summed = image_unit.astype(jnp.bfloat16)
        caption_summed = text_unit.astype(jnp.bfloat16)
        loss_total = jnp.zeros((rows,), jnp.float32)
        grad_image = jnp.zeros((rows, D), jnp.float32)
        grad_text = jnp.zeros((rows, D), jnp.float32)
        for peer_distance in range(SPAN):
            neighbor_caption = normalize(text_blocks[(index - peer_distance) % count])[0].astype(jnp.bfloat16)
            objective_total, score_multiplier = matrix_entries(picture_summed, neighbor_caption, score_scaling, score_shift, peer_distance == 0)
            loss_total = loss_total + objective_total
            grad_image = grad_image + jnp.dot(score_multiplier, neighbor_caption, preferred_element_type=jnp.float32)
            neighbor_picture = normalize(image_blocks[(index + peer_distance) % count])[0].astype(jnp.bfloat16)
            discarded_output, reverse_multiplier = matrix_entries(neighbor_picture, caption_summed, score_scaling, score_shift, peer_distance == 0)
            grad_text = grad_text + lax.dot_general(reverse_multiplier, neighbor_picture, (((0,), (0,)), ((), ())), preferred_element_type=jnp.float32)
        loss_mean = loss_total / (SPAN * rows)
        image_out = project(image_unit, grad_image, image_length).astype(jnp.bfloat16)
        text_out = project(text_unit, grad_text, text_length).astype(jnp.bfloat16)
        return (loss_mean, image_out, text_out)
    loss_rows, image_grad, text_grad = lax.map(one_block, jnp.arange(count, dtype=jnp.int32))
    return (loss_rows.reshape(PAIRS), image_grad.reshape(PAIRS, D), text_grad.reshape(PAIRS, D))
```

```python
import functools
import jax
import jax.numpy as jnp
from jax import lax
from jax.experimental import pallas as pl
from jax.experimental.pallas import tpu as pltpu
from jax.sharding import PartitionSpec as P

MESH = pl.DeviceIdType.MESH
D = 1152
ROWS = 384
SPAN = 4
R = 128
NC = ROWS // R
WIDE = 256
LOG2E = 1.4426950408889634

P1, P2, P3, Q1, Q2, Q3 = 1, 2, 3, 5, 6, 7


def digits(*order):
    code = 0
    for digit in reversed(order):
        code = code * 8 + digit
    return code


ORDER = {
    (1, 0): digits(Q2, P1, Q1, P3, Q3, P2),
    (1, 1): digits(Q2, P1, Q1, Q3, P3, P2),
    (0, 0): digits(Q2, P1, Q3, P3, Q1, P2),
    (0, 1): digits(Q2, P1, Q3, Q1, P3, P2),
}


def place(index, total):
    index = lax.rem(index + total, total)
    return (lax.div(index, 2), lax.rem(index, 2))


def entries(dots, scale, bias, sign=None):
    power = dots * (scale * LOG2E) + bias * LOG2E
    if sign is not None:
        power = power * sign
    grown = jnp.exp2(power)
    one = 1.0 + grown
    inverse = pl.reciprocal(one, approx=True)
    inverse = inverse * (2.0 - one * inverse)
    term = jnp.where(grown < 0.0078125, grown * (1.0 - grown * (0.5 - grown * (1.0 / 3.0))), jnp.log(one))
    coef = grown * inverse * scale
    if sign is not None:
        coef = coef * sign
    return term, coef.astype(jnp.bfloat16)


def lanes(term):
    folded = term[:, :R]
    for j in range(R, term.shape[1], R):
        folded = folded + term[:, j : j + R]
    return folded


def kernel(total, scaling, shift, picture, caption, loss_out, image_out, text_out,
           raw, buf, grad, loss, inv, in_sem, send_sem, recv_sem, ack):
    blk, inner_index = lax.axis_index("blk"), lax.axis_index("inner")
    me = blk * 2 + inner_index
    core = lax.rem(blk, 2)
    p = core
    q = 1 - core
    sgn = 1 - 2 * core
    outer = 1 - (core - inner_index) * (core - inner_index)

    barrier = pltpu.get_barrier_semaphore()
    for away in (1, 2, 3):
        pl.semaphore_signal(barrier, inc=1, device_id=place(me - away, total), device_id_type=MESH)

    def fetch(kind, c):
        ref = caption if kind == 0 else picture
        rows = pl.ds(c * R, R)
        return pltpu.make_async_copy(ref.at[rows], raw.at[kind, rows], in_sem.at[kind, c])

    for c in range(NC):
        for kind in (0, 1):
            fetch(kind, c).start()

    def chunk(kind, distance, c):
        start = c * R if isinstance(c, int) else pl.multiple_of(c * R, R)
        return buf.at[kind, distance, pl.ds(start, R)]

    def send(slot, kind, source, target, away, c):
        return pltpu.make_async_remote_copy(
            src_ref=chunk(kind, source, c),
            dst_ref=chunk(kind, target, c),
            send_sem=send_sem.at[slot, c],
            recv_sem=recv_sem.at[kind, target, c],
            device_id=place(me + away, total),
            device_id_type=MESH,
        )

    def s0(c):
        return send(0, p, 0, 1, sgn, c)

    def s1(c):
        return send(1, p, 0, 2, 2 * sgn, c)

    def s2(c):
        return send(2, q, 0, 1, -sgn, c)

    def s3(c):
        return send(3, p, 1, 3, 2 * sgn, c)

    def s4(c):
        return send(4, p, outer, 3 - outer, sgn * (3 - 2 * outer), c)

    def s5(c):
        return send(5, q, outer, 3 - outer, -sgn * (3 - 2 * outer), c)

    def start(*sends):
        for one in sends:
            for c in range(NC):
                one(c).start()

    for c in range(NC):
        rows = pl.ds(c * R, R)
        for kind in (0, 1):
            fetch(kind, c).wait()
            values = raw[kind, rows].astype(jnp.float32)
            shrink = 1.0 / jnp.sqrt(jnp.sum(values * values, axis=-1, keepdims=True) + 1e-06)
            inv[kind, rows] = shrink
            buf[kind, 0, rows] = (values * shrink).astype(jnp.bfloat16)

    pl.semaphore_wait(barrier, 3)
    for away in (1, 2, 3):
        pl.semaphore_signal(ack.at[away - 1], inc=1, device_id=place(me + away, total), device_id_type=MESH)

    on_first, on_second = core == 0, core == 1
    is_outer, is_inner = outer == 1, outer == 0

    @pl.when(on_first & is_outer)
    def _():
        start(s0)

    @pl.when(on_first & is_inner)
    def _():
        start(s4)

    @pl.when(on_first)
    def _():
        start(s1)

    @pl.when(on_second)
    def _():
        start(s2)

    @pl.when(on_second & is_inner)
    def _():
        start(s5)

    pl.semaphore_wait(ack.at[0], 1)

    @pl.when(on_first)
    def _():
        start(s2)

    @pl.when((on_first & is_inner) | on_second)
    def _():
        start(s0)

    scale, bias = scaling[0], shift[0]

    row = lax.broadcasted_iota(jnp.int32, (ROWS, ROWS), 0)
    col = lax.broadcasted_iota(jnp.int32, (ROWS, ROWS), 1)
    sign = jnp.where(row == col, jnp.float32(-1.0), jnp.float32(1.0))
    dots = lax.dot_general(buf[1, 0], buf[0, 0], (((1,), (1,)), ((), ())), preferred_element_type=jnp.float32)
    term, coef = entries(dots, scale, bias, sign)
    loss[0] = lanes(term)
    loss[1] = jnp.zeros((ROWS, R), jnp.float32)
    for n in range(0, D, 384):
        cols = pl.ds(n, 384)
        grad[1, :, cols] = jnp.dot(coef, buf[0, 0, :, cols], preferred_element_type=jnp.float32)
        grad[0, :, cols] = lax.dot_general(coef, buf[1, 0, :, cols], (((0,), (0,)), ((), ())), preferred_element_type=jnp.float32)

    pl.semaphore_wait(ack.at[1], 1)

    @pl.when(on_second)
    def _():
        start(s1)

    pl.semaphore_wait(ack.at[2], 1)

    @pl.when(on_first & is_inner)
    def _():
        start(s5)

    @pl.when(on_second & is_inner)
    def _():
        start(s4)

    def arrived(kind, distance, c):
        pltpu.make_async_remote_copy(
            src_ref=chunk(kind, distance, c), dst_ref=chunk(kind, distance, c),
            send_sem=send_sem.at[0, c], recv_sem=recv_sem.at[kind, distance, c],
            device_id=place(me + 1, total), device_id_type=MESH).wait_recv()

    def use(digit, first, count):
        second = lax.div(digit, 4)
        distance = lax.rem(digit, 4)
        kind = p + second * (q - p)
        other = 1 - kind
        for c in range(first, first + count):
            arrived(kind, distance, c)

            @pl.when(digit == P1)
            def _():
                s3(c).start()

            @pl.when((digit == P1) & is_outer)
            def _():
                s4(c).start()

            @pl.when((digit == Q1) & is_outer)
            def _():
                s5(c).start()

        far = buf.at[kind, distance, pl.ds(first * R, count * R)]
        dots = lax.dot_general(buf[other, 0], far[...], (((1,), (1,)), ((), ())), preferred_element_type=jnp.float32)
        term, coef = entries(dots, scale, bias)
        loss[kind] += lanes(term)
        for n in range(0, D, 384):
            cols = pl.ds(n, 384)
            grad[other, :, cols] += jnp.dot(coef, far[:, cols], preferred_element_type=jnp.float32)

    split = 2 + outer + (1 - core)

    def each(first, count):
        def body(_, code):
            use(lax.rem(code, 8), first, count)
            return lax.div(code, 8)
        return body

    code = 0
    for (o, c), value in ORDER.items():
        here = (1 - (outer - o) * (outer - o)) * (1 - (core - c) * (core - c))
        code = code + here * value

    def group(g, code):
        steps = lax.div(2 - g, 2) + lax.rem(g, 2) * split + lax.div(g, 2) * (5 - split)
        lax.fori_loop(0, steps, each(0, WIDE // R), code)
        return lax.fori_loop(0, steps, each(WIDE // R, NC - WIDE // R), code)

    lax.fori_loop(0, 3, group, code)

    for kind, ref in ((0, text_out), (1, image_out)):
        for r in range(0, ROWS, 32):
            rows = pl.ds(r, 32)
            values = raw[kind, rows].astype(jnp.float32)
            shrink = inv[kind, rows]
            whole = grad[kind, rows]
            along = jnp.sum(values * whole, axis=-1, keepdims=True) * (shrink * shrink)
            ref[rows] = ((whole - values * along) * shrink).astype(jnp.bfloat16)
    loss_out[...] = jnp.sum(loss[0].T, axis=0, keepdims=True) * (1.0 / (SPAN * ROWS))

    for c in range(NC):
        for one in (s0, s1, s2, s3, s4, s5):
            one(c).wait_send()


def local(picture, caption, scaling, shift):
    total = lax.axis_size("blk") * lax.axis_size("inner")
    vmem = pl.BlockSpec(memory_space=pltpu.VMEM)
    smem = pl.BlockSpec(memory_space=pltpu.SMEM)
    hbm = pl.BlockSpec(memory_space=pltpu.HBM)
    loss, image, text = pl.pallas_call(
        functools.partial(kernel, total),
        out_shape=(
            jax.ShapeDtypeStruct((1, ROWS), jnp.float32),
            jax.ShapeDtypeStruct((ROWS, D), jnp.bfloat16),
            jax.ShapeDtypeStruct((ROWS, D), jnp.bfloat16),
        ),
        in_specs=[smem, smem, hbm, hbm],
        out_specs=(vmem, vmem, vmem),
        scratch_shapes=[
            pltpu.VMEM((2, ROWS, D), jnp.bfloat16),
            pltpu.VMEM((2, 4, ROWS, D), jnp.bfloat16),
            pltpu.VMEM((2, ROWS, D), jnp.float32),
            pltpu.VMEM((2, ROWS, R), jnp.float32),
            pltpu.VMEM((2, ROWS, 1), jnp.float32),
            pltpu.SemaphoreType.DMA((2, NC)),
            pltpu.SemaphoreType.DMA((6, NC)),
            pltpu.SemaphoreType.DMA((2, 4, NC)),
            pltpu.SemaphoreType.REGULAR((3,)),
        ],
        compiler_params=pltpu.CompilerParams(collective_id=0, has_side_effects=True, vmem_limit_bytes=40 * 2**20),
    )(scaling.reshape(1), shift.reshape(1), picture, caption)
    return loss.reshape(ROWS), image, text


def solution(mesh):
    in_specs = (P(("blk", "inner"), None), P(("blk", "inner"), None), P(), P())
    out_specs = (P(("blk", "inner")), P(("blk", "inner"), None), P(("blk", "inner"), None))
    return jax.shard_map(local, mesh=mesh, in_specs=in_specs, out_specs=out_specs, check_vma=False)
```

```python
import functools
import jax
import jax.numpy as jnp
from jax import lax
from jax.experimental import pallas as pl
from jax.experimental.pallas import tpu as pltpu
from jax.sharding import PartitionSpec as P

MESH = pl.DeviceIdType.MESH
D = 1152
ROWS = 384
SPAN = 4
R = 128
NC = ROWS // R
WIDE = 256
LOG2E = 1.4426950408889634

P1, P2, P3, Q1, Q2, Q3 = 1, 2, 3, 5, 6, 7
LATE = 8


def packed(*items):
    codes = []
    for begin in range(0, len(items), 6):
        code = 0
        for item in reversed(items[begin : begin + 6]):
            code = code * 16 + item
        codes.append(code)
    return codes


OUTER = packed(Q2, LATE + Q2, Q1, Q3, P1, LATE + Q1, LATE + Q3, LATE + P1, P3, LATE + P3, P2, LATE + P2)
ACROSS = packed(Q2, LATE + Q2, P3, LATE + P3, P1, LATE + P1, Q3, LATE + Q3, Q1, P2, LATE + Q1, LATE + P2)
ALONG = packed(Q2, LATE + Q2, P1, LATE + P1, Q3, LATE + Q3, Q1, P2, P3, LATE + Q1, LATE + P2, LATE + P3)

EARLIEST = 2
FIRST_IN = packed(Q2, LATE + Q2, P1, LATE + P1, P3, LATE + P3, Q1, LATE + Q1, P2, Q3, LATE + Q3, LATE + P2)


def place(index, total):
    index = lax.rem(index + total, total)
    return (lax.div(index, 2), lax.rem(index, 2))


def entries(dots, scale, bias, sign=None):
    power = dots * (scale * LOG2E) + bias * LOG2E
    if sign is not None:
        power = power * sign
    grown = jnp.exp2(power)
    one = 1.0 + grown
    inverse = pl.reciprocal(one, approx=True)
    inverse = inverse * (2.0 - one * inverse)
    term = jnp.where(grown < 0.0078125, grown * (1.0 - grown * (0.5 - grown * (1.0 / 3.0))), jnp.log(one))
    coef = grown * inverse * scale
    if sign is not None:
        coef = coef * sign
    return term, coef.astype(jnp.bfloat16)


def lanes(term):
    folded = term[:, :R]
    for j in range(R, term.shape[1], R):
        folded = folded + term[:, j : j + R]
    return folded


def kernel(total, scaling_in, shift_in, picture, caption, loss_out, image_out, text_out,
           raw, buf, grad, loss, inv, in_sem, send_sem, recv_sem, ack, scalars, scalar_sem):
    blk, inner_index = lax.axis_index("blk"), lax.axis_index("inner")
    me = blk * 2 + inner_index
    core = lax.rem(blk, 2)
    p = core
    q = 1 - core
    sgn = 1 - 2 * core
    outer = 1 - (core - inner_index) * (core - inner_index)

    barrier = pltpu.get_barrier_semaphore()
    for away in (1, 2, 3):
        pl.semaphore_signal(barrier, inc=1, device_id=place(me - away, total), device_id_type=MESH)

    fetch_scalars = [
        pltpu.make_async_copy(ref, scalars.at[i], scalar_sem.at[i]) for i, ref in enumerate((scaling_in, shift_in))
    ]
    for one in fetch_scalars:
        one.start()

    def fetch(kind, c):
        ref = caption if kind == 0 else picture
        rows = pl.ds(c * R, R)
        return pltpu.make_async_copy(ref.at[rows], raw.at[kind, rows], in_sem.at[kind, c])

    for c in range(NC):
        for kind in (0, 1):
            fetch(kind, c).start( )

    def chunk(kind, distance, c):
        start = c * R if isinstance(c, int) else pl.multiple_of(c * R, R)
        return buf.at[kind, distance, pl.ds(start, R)]

    def send(slot, kind, source, target, away, c):
        return pltpu.make_async_remote_copy(
            src_ref=chunk(kind, source, c),
            dst_ref=chunk(kind, target, c),
            send_sem=send_sem.at[slot, c],
            recv_sem=recv_sem.at[kind, target, c],
            device_id=place(me + away, total),
            device_id_type=MESH,
        )

    def s0(c):
        return send(0, p, 0, 1, sgn, c)

    def s1(c):
        return send(1, p, 0, 2, 2 * sgn, c)

    def s2(c):
        return send(2, q, 0, 1, -sgn, c)

    def s3(c):
        return send(3, p, 1, 3, 2 * sgn, c)

    def s4(c):
        return send(4, p, outer, 3 - outer, sgn * (3 - 2 * outer), c)

    def s5(c):
        return send(5, q, outer, 3 - outer, -sgn * (3 - 2 * outer), c)

    def start(*sends):
        for one in sends:
            for c in range(NC):
                one(c).start()

    def normalize(kind, c):
        fetch(kind, c).wait()
        rows = pl.ds(c * R, R)
        values = raw[kind, rows].astype(jnp.float32)
        shrink = 1.0 / jnp.sqrt(jnp.sum(values * values, axis=-1, keepdims=True) + 1e-06)
        inv[kind, rows] = shrink
        buf[kind, 0, rows] = (values * shrink).astype(jnp.bfloat16)

    high = lax.rem(lax.div(blk, 2), 2)
    along = (high - core) * (high - core)
    on_first, on_second = core == 0, core == 1
    is_outer, is_inner = outer == 1, outer == 0

    for c in range(NC):
        normalize(0, c)
        if c == 0:
            pl.semaphore_wait(barrier, 3)
            for away in (1, 2, 3):
                pl.semaphore_signal(ack.at[away - 1], inc=1, device_id=place(me + away, total), device_id_type=MESH)

        @pl.when(on_first & is_outer)
        def _():
            s0(c).start()

        @pl.when(on_first & is_inner & (along == 0))
        def _():
            s4(c).start()

        @pl.when(on_second)
        def _():
            s2(c).start()

        normalize(1, c)

    @pl.when(on_second & is_inner)
    def _():
        start(s5)

    @pl.when(on_first)
    def _():
        start(s1)

    ahead_first = me == EARLIEST - 1

    @pl.when(ahead_first)
    def _():
        start(s0)

    pl.semaphore_wait(ack.at[0], 1)

    @pl.when(on_first)
    def _():
        start(s2)

    @pl.when((on_first & is_inner & jnp.logical_not(ahead_first)) | on_second)
    def _():
        start(s0)

    third_now = is_inner & on_first & (along == 1)

    @pl.when(third_now)
    def _():
        pl.semaphore_wait(ack.at[2], 1)
        start(s5)

    for one in fetch_scalars:
        one.wait()
    scale, bias = scalars[0, 0], scalars[1, 0]

    row = lax.broadcasted_iota(jnp.int32, (ROWS, ROWS), 0)
    col = lax.broadcasted_iota(jnp.int32, (ROWS, ROWS), 1)
    sign = jnp.where(row == col, jnp.float32(-1.0), jnp.float32(1.0))
    dots = lax.dot_general(buf[1, 0], buf[0, 0], (((1,), (1,)), ((), ())), preferred_element_type=jnp.float32)
    term, coef = entries(dots, scale, bias, sign)
    loss[0] = lanes(term)
    loss[1] = jnp.zeros((ROWS, R), jnp.float32)
    for n in range(0, D, 384):
        cols = pl.ds(n, 384)
        grad[1, :, cols] = jnp.dot(coef, buf[0, 0, :, cols], preferred_element_type=jnp.float32)
        grad[0, :, cols] = lax.dot_general(coef, buf[1, 0, :, cols], (((0,), (0,)), ((), ())), preferred_element_type=jnp.float32)

    pl.semaphore_wait(ack.at[1], 1)

    @pl.when(on_second)
    def _():
        start(s1)

    def late_sends():
        @pl.when(jnp.logical_not(third_now))
        def _():
            pl.semaphore_wait(ack.at[2], 1)

        @pl.when(is_inner & ((along == 1) | on_second))
        def _():
            start(s4)

        @pl.when(is_inner & on_first & (along == 0))
        def _():
            start(s5)

    def arrived(kind, distance, c):
        pltpu.make_async_remote_copy(
            src_ref=chunk(kind, distance, c), dst_ref=chunk(kind, distance, c),
            send_sem=send_sem.at[0, c], recv_sem=recv_sem.at[kind, distance, c],
            device_id=place(me + 1, total), device_id_type=MESH).wait_recv()

    def use(block, first, count):
        second = lax.div(block, 4)
        distance = lax.rem(block, 4)
        kind = p + second * (q - p)
        other = 1 - kind
        for c in range(first, first + count):
            arrived(kind, distance, c)

            @pl.when(block == P1)
            def _():
                s3(c).start()

            @pl.when((block == P1) & is_outer)
            def _():
                s4(c).start()

            @pl.when((block == Q1) & is_outer)
            def _():
                s5(c).start()

        far = buf.at[kind, distance, pl.ds(first * R, count * R)]
        dots = lax.dot_general(buf[other, 0], far[...], (((1,), (1,)), ((), ())), preferred_element_type=jnp.float32)
        term, coef = entries(dots, scale, bias)
        loss[kind] += lanes(term)
        for n in range(0, D, 384):
            cols = pl.ds(n, 384)
            grad[other, :, cols] += jnp.dot(coef, far[:, cols], preferred_element_type=jnp.float32)

    for half in (0, 1):
        code = outer * OUTER[half] + (1 - outer) * (along * ALONG[half] + (1 - along) * ACROSS[half])
        code = jnp.where(me == EARLIEST, FIRST_IN[half], code)

        def step(i, code):
            item = lax.rem(code, 16)

            if half == 0:
                pl.when(i == 2)(late_sends)

            @pl.when(item < LATE)
            def _():
                use(item, 0, WIDE // R)

            @pl.when(item >= LATE)
            def _():
                use(item - LATE, WIDE // R, NC - WIDE // R)

            return lax.div(code, 16)

        lax.fori_loop(0, 6, step, code)

    for kind, ref in ((0, text_out), (1, image_out)):
        for r in range(0, ROWS, 32):
            rows = pl.ds(r, 32)
            values = raw[kind, rows].astype(jnp.float32)
            shrink = inv[kind, rows]
            whole = grad[kind, rows]
            along = jnp.sum(values * whole, axis=-1, keepdims=True) * (shrink * shrink)
            ref[rows] = ((whole - values * along) * shrink).astype(jnp.bfloat16)
    loss_out[...] = jnp.sum(loss[0].T, axis=0, keepdims=True) * (1.0 / (SPAN * ROWS))

    for c in range(NC):
        for one in (s0, s1, s2, s3, s4, s5):
            one(c).wait_send()


def local(picture, caption, scaling, shift):
    total = lax.axis_size("blk") * lax.axis_size("inner")
    vmem = pl.BlockSpec(memory_space=pltpu.VMEM)
    hbm = pl.BlockSpec(memory_space=pltpu.HBM)
    picture = pltpu.with_memory_space_constraint(picture, pltpu.HBM)
    caption = pltpu.with_memory_space_constraint(caption, pltpu.HBM)
    results = pl.pallas_call(
        functools.partial(kernel, total),
        out_shape=(
            jax.ShapeDtypeStruct((1, ROWS), jnp.float32),
            jax.ShapeDtypeStruct((ROWS, D), jnp.bfloat16),
            jax.ShapeDtypeStruct((ROWS, D), jnp.bfloat16),
        ),
        in_specs=[hbm] * 4,
        out_specs=(vmem, vmem, vmem),
        scratch_shapes=[
            pltpu.VMEM((2, ROWS, D), jnp.bfloat16),
            pltpu.VMEM((2, 4, ROWS, D), jnp.bfloat16),
            pltpu.VMEM((2, ROWS, D), jnp.float32),
            pltpu.VMEM((2, ROWS, R), jnp.float32),
            pltpu.VMEM((2, ROWS, 1), jnp.float32),
            pltpu.SemaphoreType.DMA((2, NC)),
            pltpu.SemaphoreType.DMA((6, NC)),
            pltpu.SemaphoreType.DMA((2, 4, NC)),
            pltpu.SemaphoreType.REGULAR((3,)),
            pltpu.SMEM((2, 1), jnp.float32),
            pltpu.SemaphoreType.DMA((2,)),
        ],
        compiler_params=pltpu.CompilerParams(collective_id=0, has_side_effects=True, vmem_limit_bytes=40 * 2**20),
    )(scaling.reshape(1), shift.reshape(1), picture, caption)
    loss, image, text = results
    return loss.reshape(ROWS), image, text


def solution(mesh):
    in_specs = (P(("blk", "inner"), None), P(("blk", "inner"), None), P(), P())
    out_specs = (P(("blk", "inner")), P(("blk", "inner"), None), P(("blk", "inner"), None))
    return jax.shard_map(local, mesh=mesh, in_specs=in_specs, out_specs=out_specs, check_vma=False)
```

```python
import functools
import jax
import jax.numpy as jnp
from jax import lax
from jax.experimental import pallas as pl
from jax.experimental.pallas import tpu as pltpu
from jax.sharding import PartitionSpec as P

MESH = pl.DeviceIdType.MESH
D = 1152
ROWS = 384
SPAN = 4
R = 128
NC = ROWS // R
WIDE = 256
LOG2E = 1.4426950408889634

P1, P2, P3, Q1, Q2, Q3 = 1, 2, 3, 5, 6, 7
LATE = 8


def packed(*items):
    codes = []
    for begin in range(0, len(items), 6):
        code = 0
        for item in reversed(items[begin : begin + 6]):
            code = code * 16 + item
        codes.append(code)
    return codes


OUTER = packed(Q2, LATE + Q2, Q1, Q3, P1, LATE + Q1, LATE + Q3, LATE + P1, P3, LATE + P3, P2, LATE + P2)
ACROSS = packed(Q2, LATE + Q2, P3, LATE + P3, P1, LATE + P1, Q3, LATE + Q3, Q1, P2, LATE + Q1, LATE + P2)
ALONG = packed(Q2, LATE + Q2, P1, LATE + P1, Q3, LATE + Q3, Q1, P2, P3, LATE + Q1, LATE + P2, LATE + P3)

EARLIEST = 2
FIRST_IN = packed(Q2, LATE + Q2, P1, LATE + P1, P3, LATE + P3, Q1, LATE + Q1, P2, Q3, LATE + Q3, LATE + P2)


def place(index, total):
    index = lax.rem(index + total, total)
    return (lax.div(index, 2), lax.rem(index, 2))


def entries(dots, scale, bias, sign=None):
    power = dots * (scale * LOG2E) + bias * LOG2E
    if sign is not None:
        power = power * sign
    grown = jnp.exp2(power)
    one = 1.0 + grown
    inverse = pl.reciprocal(one, approx=True)
    inverse = inverse * (2.0 - one * inverse)
    term = jnp.where(grown < 0.0078125, grown * (1.0 - grown * (0.5 - grown * (1.0 / 3.0))), jnp.log(one))
    coef = grown * inverse * scale
    if sign is not None:
        coef = coef * sign
    return term, coef.astype(jnp.bfloat16)


def lanes(term):
    folded = term[:, :R]
    for j in range(R, term.shape[1], R):
        folded = folded + term[:, j : j + R]
    return folded


def kernel(total, scaling_in, shift_in, picture, caption, loss_out, image_out, text_out,
           raw, buf, grad, loss, inv, in_sem, send_sem, recv_sem, ack):
    blk, inner_index = lax.axis_index("blk"), lax.axis_index("inner")
    me = blk * 2 + inner_index
    core = lax.rem(blk, 2)
    p = core
    q = 1 - core
    sgn = 1 - 2 * core
    outer = 1 - (core - inner_index) * (core - inner_index)

    barrier = pltpu.get_barrier_semaphore()
    for away in (1, 2, 3):
        pl.semaphore_signal(barrier, inc=1, device_id=place(me - away, total), device_id_type=MESH)

    def fetch(kind, c):
        ref = caption if kind == 0 else picture
        rows = pl.ds(c * R, R)
        return pltpu.make_async_copy(ref.at[rows], raw.at[kind, rows], in_sem.at[kind, c])

    for c in range(NC):
        for kind in (0, 1):
            fetch(kind, c).start( )

    def chunk(kind, distance, c):
        start = c * R if isinstance(c, int) else pl.multiple_of(c * R, R)
        return buf.at[kind, distance, pl.ds(start, R)]

    def send(slot, kind, source, target, away, c):
        return pltpu.make_async_remote_copy(
            src_ref=chunk(kind, source, c),
            dst_ref=chunk(kind, target, c),
            send_sem=send_sem.at[slot, c],
            recv_sem=recv_sem.at[kind, target, c],
            device_id=place(me + away, total),
            device_id_type=MESH,
        )

    def s0(c):
        return send(0, p, 0, 1, sgn, c)

    def s1(c):
        return send(1, p, 0, 2, 2 * sgn, c)

    def s2(c):
        return send(2, q, 0, 1, -sgn, c)

    def s3(c):
        return send(3, p, 1, 3, 2 * sgn, c)

    def s4(c):
        return send(4, p, outer, 3 - outer, sgn * (3 - 2 * outer), c)

    def s5(c):
        return send(5, q, outer, 3 - outer, -sgn * (3 - 2 * outer), c)

    def start(*sends):
        for one in sends:
            for c in range(NC):
                one(c).start()

    def normalize(kind, c):
        fetch(kind, c).wait()
        rows = pl.ds(c * R, R)
        values = raw[kind, rows].astype(jnp.float32)
        shrink = 1.0 / jnp.sqrt(jnp.sum(values * values, axis=-1, keepdims=True) + 1e-06)
        inv[kind, rows] = shrink
        buf[kind, 0, rows] = (values * shrink).astype(jnp.bfloat16)

    high = lax.rem(lax.div(blk, 2), 2)
    along = (high - core) * (high - core)
    on_first, on_second = core == 0, core == 1
    is_outer, is_inner = outer == 1, outer == 0

    for c in range(NC):
        normalize(0, c)
        if c == 0:
            pl.semaphore_wait(barrier, 3)
            for away in (1, 2, 3):
                pl.semaphore_signal(ack.at[away - 1], inc=1, device_id=place(me + away, total), device_id_type=MESH)

        @pl.when(on_first & is_outer)
        def _():
            s0(c).start()

        @pl.when(on_first & is_inner & (along == 0))
        def _():
            s4(c).start()

        @pl.when(on_second)
        def _():
            s2(c).start()

        normalize(1, c)

    @pl.when(on_second & is_inner)
    def _():
        start(s5)

    @pl.when(on_first)
    def _():
        start(s1)

    ahead_first = me == EARLIEST - 1

    @pl.when(ahead_first)
    def _():
        start(s0)

    pl.semaphore_wait(ack.at[0], 1)

    @pl.when(on_first)
    def _():
        start(s2)

    @pl.when((on_first & is_inner & jnp.logical_not(ahead_first)) | on_second)
    def _():
        start(s0)

    third_now = is_inner & on_first & (along == 1)

    @pl.when(third_now)
    def _():
        pl.semaphore_wait(ack.at[2], 1)
        start(s5)

    scale, bias = scaling_in[:1, :1], shift_in[:1, :1]

    row = lax.broadcasted_iota(jnp.int32, (ROWS, ROWS), 0)
    col = lax.broadcasted_iota(jnp.int32, (ROWS, ROWS), 1)
    sign = jnp.where(row == col, jnp.float32(-1.0), jnp.float32(1.0))
    dots = lax.dot_general(buf[1, 0], buf[0, 0], (((1,), (1,)), ((), ())), preferred_element_type=jnp.float32)
    term, coef = entries(dots, scale, bias, sign)
    loss[0] = lanes(term)
    loss[1] = jnp.zeros((ROWS, R), jnp.float32)
    for n in range(0, D, 384):
        cols = pl.ds(n, 384)
        grad[1, :, cols] = jnp.dot(coef, buf[0, 0, :, cols], preferred_element_type=jnp.float32)
        grad[0, :, cols] = lax.dot_general(coef, buf[1, 0, :, cols], (((0,), (0,)), ((), ())), preferred_element_type=jnp.float32)

    pl.semaphore_wait(ack.at[1], 1)

    @pl.when(on_second)
    def _():
        start(s1)

    def late_sends():
        @pl.when(jnp.logical_not(third_now))
        def _():
            pl.semaphore_wait(ack.at[2], 1)

        @pl.when(is_inner & ((along == 1) | on_second))
        def _():
            start(s4)

        @pl.when(is_inner & on_first & (along == 0))
        def _():
            start(s5)

    def arrived(kind, distance, c):
        pltpu.make_async_remote_copy(
            src_ref=chunk(kind, distance, c), dst_ref=chunk(kind, distance, c),
            send_sem=send_sem.at[0, c], recv_sem=recv_sem.at[kind, distance, c],
            device_id=place(me + 1, total), device_id_type=MESH).wait_recv()

    def use(block, first, count):
        second = lax.div(block, 4)
        distance = lax.rem(block, 4)
        kind = p + second * (q - p)
        other = 1 - kind
        for c in range(first, first + count):
            arrived(kind, distance, c)

            @pl.when(block == P1)
            def _():
                s3(c).start()

            @pl.when((block == P1) & is_outer)
            def _():
                s4(c).start()

            @pl.when((block == Q1) & is_outer)
            def _():
                s5(c).start()

        far = buf.at[kind, distance, pl.ds(first * R, count * R)]
        dots = lax.dot_general(buf[other, 0], far[...], (((1,), (1,)), ((), ())), preferred_element_type=jnp.float32)
        term, coef = entries(dots, scale, bias)
        loss[kind] += lanes(term)
        for n in range(0, D, 384):
            cols = pl.ds(n, 384)
            grad[other, :, cols] += jnp.dot(coef, far[:, cols], preferred_element_type=jnp.float32)

    for half in (0, 1):
        code = outer * OUTER[half] + (1 - outer) * (along * ALONG[half] + (1 - along) * ACROSS[half])
        code = jnp.where(me == EARLIEST, FIRST_IN[half], code)

        def step(i, code):
            item = lax.rem(code, 16)

            if half == 0:
                pl.when(i == 2)(late_sends)

            @pl.when(item < LATE)
            def _():
                use(item, 0, WIDE // R)

            @pl.when(item >= LATE)
            def _():
                use(item - LATE, WIDE // R, NC - WIDE // R)

            return lax.div(code, 16)

        lax.fori_loop(0, 6, step, code)

    for kind, ref in ((0, text_out), (1, image_out)):
        for r in range(0, ROWS, 32):
            rows = pl.ds(r, 32)
            values = raw[kind, rows].astype(jnp.float32)
            shrink = inv[kind, rows]
            whole = grad[kind, rows]
            along = jnp.sum(values * whole, axis=-1, keepdims=True) * (shrink * shrink)
            ref[rows] = ((whole - values * along) * shrink).astype(jnp.bfloat16)
    loss_out[...] = jnp.sum(loss[0].T, axis=0, keepdims=True) * (1.0 / (SPAN * ROWS))

    for c in range(NC):
        for one in (s0, s1, s2, s3, s4, s5):
            one(c).wait_send()


def hand_over(loss, image, text, loss_out, image_out, text_out, sem):
    copies = [
        pltpu.make_async_copy(source, target, sem.at[i])
        for i, (source, target) in enumerate(((image, image_out), (text, text_out)))
    ]
    for copy in copies:
        copy.start()
    loss_out[...] = loss[0]
    for copy in copies:
        copy.wait()


def local(picture, caption, scaling, shift):
    total = lax.axis_size("blk") * lax.axis_size("inner")
    vmem = pl.BlockSpec(memory_space=pltpu.VMEM)
    hbm = pl.BlockSpec(memory_space=pltpu.HBM)
    picture = pltpu.with_memory_space_constraint(picture, pltpu.HBM)
    caption = pltpu.with_memory_space_constraint(caption, pltpu.HBM)
    results = pl.pallas_call(
        functools.partial(kernel, total),
        out_shape=(
            jax.ShapeDtypeStruct((1, ROWS), jnp.float32),
            jax.ShapeDtypeStruct((ROWS, D), jnp.bfloat16),
            jax.ShapeDtypeStruct((ROWS, D), jnp.bfloat16),
        ),
        in_specs=[vmem, vmem, hbm, hbm],
        out_specs=(vmem, vmem, vmem),
        scratch_shapes=[
            pltpu.VMEM((2, ROWS, D), jnp.bfloat16),
            pltpu.VMEM((2, 4, ROWS, D), jnp.bfloat16),
            pltpu.VMEM((2, ROWS, D), jnp.float32),
            pltpu.VMEM((2, ROWS, R), jnp.float32),
            pltpu.VMEM((2, ROWS, 1), jnp.float32),
            pltpu.SemaphoreType.DMA((2, NC)),
            pltpu.SemaphoreType.DMA((6, NC)),
            pltpu.SemaphoreType.DMA((2, 4, NC)),
            pltpu.SemaphoreType.REGULAR((3,)),
        ],
        compiler_params=pltpu.CompilerParams(collective_id=0, allow_input_fusion=[True, True, False, False], has_side_effects=True, vmem_limit_bytes=40 * 2**20),
    )(jnp.full((8, 128), scaling), jnp.full((8, 128), shift), picture, caption)
    anywhere = pl.BlockSpec(memory_space=pl.ANY)
    loss, image, text = pl.pallas_call(
        hand_over,
        out_shape=(
            jax.ShapeDtypeStruct((ROWS,), jnp.float32),
            jax.ShapeDtypeStruct((ROWS, D), jnp.bfloat16),
            jax.ShapeDtypeStruct((ROWS, D), jnp.bfloat16),
        ),
        in_specs=[vmem, anywhere, anywhere],
        out_specs=(vmem, hbm, hbm),
        scratch_shapes=[pltpu.SemaphoreType.DMA((2,))],
        compiler_params=pltpu.CompilerParams(vmem_limit_bytes=2**20),
        name="hand_over",
    )(*results)
    return loss, image, text


def solution(mesh):
    in_specs = (P(("blk", "inner"), None), P(("blk", "inner"), None), P(), P())
    out_specs = (P(("blk", "inner")), P(("blk", "inner"), None), P(("blk", "inner"), None))
    return jax.shard_map(local, mesh=mesh, in_specs=in_specs, out_specs=out_specs, check_vma=False)
```

```python
import functools
import jax
import jax.numpy as jnp
from jax import lax
from jax.experimental import pallas as pl
from jax.experimental.pallas import tpu as pltpu
from jax.sharding import PartitionSpec as P

MESH = pl.DeviceIdType.MESH
D = 1152
ROWS = 384
SPAN = 4
R = 128
NC = ROWS // R
WIDE = 256
LOG2E = 1.4426950408889634

P1, P2, P3, Q1, Q2, Q3 = 1, 2, 3, 5, 6, 7
LATE = 8


def packed(*items):
    codes = []
    for begin in range(0, len(items), 6):
        code = 0
        for item in reversed(items[begin : begin + 6]):
            code = code * 16 + item
        codes.append(code)
    return codes


OUTER = packed(Q2, LATE + Q2, Q1, Q3, P1, LATE + Q1, LATE + Q3, LATE + P1, P3, LATE + P3, P2, LATE + P2)
ACROSS = packed(Q2, LATE + Q2, P3, LATE + P3, P1, LATE + P1, Q3, LATE + Q3, Q1, P2, LATE + Q1, LATE + P2)
ALONG = packed(Q2, LATE + Q2, P1, LATE + P1, Q3, LATE + Q3, Q1, P2, P3, LATE + Q1, LATE + P2, LATE + P3)

EARLIEST = 2
FIRST_IN = packed(Q2, LATE + Q2, P1, LATE + P1, P3, LATE + P3, Q1, LATE + Q1, P2, Q3, LATE + Q3, LATE + P2)

ORIGIN = packed(Q2, LATE + Q2, Q3, P1, LATE + Q3, LATE + P1, P3, Q1, LATE + P3, LATE + Q1, P2, LATE + P2)

FOURTH = packed(Q2, LATE + Q2, Q1, P1, LATE + Q1, P3, Q3, LATE + P1, LATE + Q3, LATE + P3, P2, LATE + P2)


def place(index, total):
    index = lax.rem(index + total, total)
    return (lax.div(index, 2), lax.rem(index, 2))


def entries(dots, scale, bias, sign=None):
    power = dots * (scale * LOG2E) + bias * LOG2E
    if sign is not None:
        power = power * sign
    grown = jnp.exp2(power)
    one = 1.0 + grown
    inverse = pl.reciprocal(one, approx=True)
    inverse = inverse * (2.0 - one * inverse)
    term = jnp.where(grown < 0.0078125, grown * (1.0 - grown * (0.5 - grown * (1.0 / 3.0))), jnp.log(one))
    coef = grown * inverse * scale
    if sign is not None:
        coef = coef * sign
    return term, coef.astype(jnp.bfloat16)


def lanes(term):
    folded = term[:, :R]
    for j in range(R, term.shape[1], R):
        folded = folded + term[:, j : j + R]
    return folded


def kernel(total, scaling_in, shift_in, picture, caption, loss_out, image_out, text_out,
           raw, buf, grad, loss, inv, in_sem, send_sem, recv_sem, ack):
    blk, inner_index = lax.axis_index("blk"), lax.axis_index("inner")
    me = blk * 2 + inner_index
    core = lax.rem(blk, 2)
    p = core
    q = 1 - core
    sgn = 1 - 2 * core
    outer = 1 - (core - inner_index) * (core - inner_index)

    barrier = pltpu.get_barrier_semaphore()
    for away in (1, 2, 3):
        pl.semaphore_signal(barrier, inc=1, device_id=place(me - away, total), device_id_type=MESH)

    def fetch(kind, c):
        ref = caption if kind == 0 else picture
        rows = pl.ds(c * R, R)
        return pltpu.make_async_copy(ref.at[rows], raw.at[kind, rows], in_sem.at[kind, c])

    for c in range(NC):
        for kind in (0, 1):
            fetch(kind, c).start( )

    def chunk(kind, distance, c):
        start = c * R if isinstance(c, int) else pl.multiple_of(c * R, R)
        return buf.at[kind, distance, pl.ds(start, R)]

    def send(slot, kind, source, target, away, c):
        return pltpu.make_async_remote_copy(
            src_ref=chunk(kind, source, c),
            dst_ref=chunk(kind, target, c),
            send_sem=send_sem.at[slot, c],
            recv_sem=recv_sem.at[kind, target, c],
            device_id=place(me + away, total),
            device_id_type=MESH,
        )

    def s0(c):
        return send(0, p, 0, 1, sgn, c)

    def s1(c):
        return send(1, p, 0, 2, 2 * sgn, c)

    def s2(c):
        return send(2, q, 0, 1, -sgn, c)

    def s3(c):
        return send(3, p, 1, 3, 2 * sgn, c)

    def s4(c):
        return send(4, p, outer, 3 - outer, sgn * (3 - 2 * outer), c)

    def s5(c):
        return send(5, q, outer, 3 - outer, -sgn * (3 - 2 * outer), c)

    def start(*sends):
        for one in sends:
            for c in range(NC):
                one(c).start()

    def normalize(kind, c):
        fetch(kind, c).wait()
        rows = pl.ds(c * R, R)
        values = raw[kind, rows].astype(jnp.float32)
        shrink = 1.0 / jnp.sqrt(jnp.sum(values * values, axis=-1, keepdims=True) + 1e-06)
        inv[kind, rows] = shrink
        buf[kind, 0, rows] = (values * shrink).astype(jnp.bfloat16)

    high = lax.rem(lax.div(blk, 2), 2)
    along = (high - core) * (high - core)
    on_first, on_second = core == 0, core == 1
    is_outer, is_inner = outer == 1, outer == 0

    for c in range(NC):
        normalize(0, c)
        if c == 0:
            pl.semaphore_wait(barrier, 3)
            for away in (1, 2, 3):
                pl.semaphore_signal(ack.at[away - 1], inc=1, device_id=place(me + away, total), device_id_type=MESH)

        @pl.when(on_first & is_outer)
        def _():
            s0(c).start()

        @pl.when(on_first & is_inner & (along == 0))
        def _():
            s4(c).start()

        @pl.when(on_second)
        def _():
            s2(c).start()

        normalize(1, c)

    @pl.when(on_second & is_inner)
    def _():
        start(s5)

    @pl.when(on_first)
    def _():
        start(s1)

    ahead_first = me == EARLIEST - 1

    @pl.when(ahead_first)
    def _():
        start(s0)

    pl.semaphore_wait(ack.at[0], 1)

    @pl.when(on_first)
    def _():
        start(s2)

    @pl.when((on_first & is_inner & jnp.logical_not(ahead_first)) | on_second)
    def _():
        start(s0)

    third_now = is_inner & on_first & (along == 1)

    @pl.when(third_now)
    def _():
        pl.semaphore_wait(ack.at[2], 1)
        start(s5)

    scale, bias = scaling_in[:1, :1], shift_in[:1, :1]

    row = lax.broadcasted_iota(jnp.int32, (ROWS, ROWS), 0)
    col = lax.broadcasted_iota(jnp.int32, (ROWS, ROWS), 1)
    sign = jnp.where(row == col, jnp.float32(-1.0), jnp.float32(1.0))
    dots = lax.dot_general(buf[1, 0], buf[0, 0], (((1,), (1,)), ((), ())), preferred_element_type=jnp.float32)
    term, coef = entries(dots, scale, bias, sign)
    loss[0] = lanes(term)
    loss[1] = jnp.zeros((ROWS, R), jnp.float32)
    for n in range(0, D, 384):
        cols = pl.ds(n, 384)
        grad[1, :, cols] = jnp.dot(coef, buf[0, 0, :, cols], preferred_element_type=jnp.float32)
        grad[0, :, cols] = lax.dot_general(coef, buf[1, 0, :, cols], (((0,), (0,)), ((), ())), preferred_element_type=jnp.float32)

    pl.semaphore_wait(ack.at[1], 1)

    @pl.when(on_second)
    def _():
        start(s1)

    def late_sends():
        @pl.when(jnp.logical_not(third_now))
        def _():
            pl.semaphore_wait(ack.at[2], 1)

        @pl.when(is_inner & ((along == 1) | on_second))
        def _():
            start(s4)

        @pl.when(is_inner & on_first & (along == 0))
        def _():
            start(s5)

    def arrived(kind, distance, c):
        pltpu.make_async_remote_copy(
            src_ref=chunk(kind, distance, c), dst_ref=chunk(kind, distance, c),
            send_sem=send_sem.at[0, c], recv_sem=recv_sem.at[kind, distance, c],
            device_id=place(me + 1, total), device_id_type=MESH).wait_recv()

    def use(block, first, count):
        second = lax.div(block, 4)
        distance = lax.rem(block, 4)
        kind = p + second * (q - p)
        other = 1 - kind
        for c in range(first, first + count):
            arrived(kind, distance, c)

            @pl.when(block == P1)
            def _():
                s3(c).start()

            @pl.when((block == P1) & is_outer)
            def _():
                s4(c).start()

            @pl.when((block == Q1) & is_outer)
            def _():
                s5(c).start()

        far = buf.at[kind, distance, pl.ds(first * R, count * R)]
        dots = lax.dot_general(buf[other, 0], far[...], (((1,), (1,)), ((), ())), preferred_element_type=jnp.float32)
        term, coef = entries(dots, scale, bias)
        loss[kind] += lanes(term)
        for n in range(0, D, 384):
            cols = pl.ds(n, 384)
            grad[other, :, cols] += jnp.dot(coef, far[:, cols], preferred_element_type=jnp.float32)

    for half in (0, 1):
        code = outer * OUTER[half] + (1 - outer) * (along * ALONG[half] + (1 - along) * ACROSS[half])
        code = jnp.where(me == EARLIEST, FIRST_IN[half], jnp.where(me == 0, ORIGIN[half], jnp.where(me == 3, FOURTH[half], code)))

        def step(i, code):
            item = lax.rem(code, 16)

            if half == 0:
                pl.when(i == 2)(late_sends)

            @pl.when(item < LATE)
            def _():
                use(item, 0, WIDE // R)

            @pl.when(item >= LATE)
            def _():
                use(item - LATE, WIDE // R, NC - WIDE // R)

            return lax.div(code, 16)

        lax.fori_loop(0, 6, step, code)

    for kind, ref in ((0, text_out), (1, image_out)):
        for r in range(0, ROWS, 32):
            rows = pl.ds(r, 32)
            values = raw[kind, rows].astype(jnp.float32)
            shrink = inv[kind, rows]
            whole = grad[kind, rows]
            along = jnp.sum(values * whole, axis=-1, keepdims=True) * (shrink * shrink)
            ref[rows] = ((whole - values * along) * shrink).astype(jnp.bfloat16)
    loss_out[...] = jnp.sum(loss[0].T, axis=0, keepdims=True) * (1.0 / (SPAN * ROWS))

    for c in range(NC):
        for one in (s0, s1, s2, s3, s4, s5):
            one(c).wait_send()


def hand_over(loss, image, text, loss_out, image_out, text_out, sem):
    copies = [
        pltpu.make_async_copy(source, target, sem.at[i])
        for i, (source, target) in enumerate(((image, image_out), (text, text_out)))
    ]
    for copy in copies:
        copy.start()
    loss_out[...] = loss[0]
    for copy in copies:
        copy.wait()


def local(picture, caption, scaling, shift):
    total = lax.axis_size("blk") * lax.axis_size("inner")
    vmem = pl.BlockSpec(memory_space=pltpu.VMEM)
    hbm = pl.BlockSpec(memory_space=pltpu.HBM)
    picture = pltpu.with_memory_space_constraint(picture, pltpu.HBM)
    caption = pltpu.with_memory_space_constraint(caption, pltpu.HBM)
    results = pl.pallas_call(
        functools.partial(kernel, total),
        out_shape=(
            jax.ShapeDtypeStruct((1, ROWS), jnp.float32),
            jax.ShapeDtypeStruct((ROWS, D), jnp.bfloat16),
            jax.ShapeDtypeStruct((ROWS, D), jnp.bfloat16),
        ),
        in_specs=[vmem, vmem, hbm, hbm],
        out_specs=(vmem, vmem, vmem),
        scratch_shapes=[
            pltpu.VMEM((2, ROWS, D), jnp.bfloat16),
            pltpu.VMEM((2, 4, ROWS, D), jnp.bfloat16),
            pltpu.VMEM((2, ROWS, D), jnp.float32),
            pltpu.VMEM((2, ROWS, R), jnp.float32),
            pltpu.VMEM((2, ROWS, 1), jnp.float32),
            pltpu.SemaphoreType.DMA((2, NC)),
            pltpu.SemaphoreType.DMA((6, NC)),
            pltpu.SemaphoreType.DMA((2, 4, NC)),
            pltpu.SemaphoreType.REGULAR((3,)),
        ],
        compiler_params=pltpu.CompilerParams(collective_id=0, allow_input_fusion=[True, True, False, False], has_side_effects=True, vmem_limit_bytes=40 * 2**20),
    )(jnp.full((8, 128), scaling), jnp.full((8, 128), shift), picture, caption)
    anywhere = pl.BlockSpec(memory_space=pl.ANY)
    loss, image, text = pl.pallas_call(
        hand_over,
        out_shape=(
            jax.ShapeDtypeStruct((ROWS,), jnp.float32),
            jax.ShapeDtypeStruct((ROWS, D), jnp.bfloat16),
            jax.ShapeDtypeStruct((ROWS, D), jnp.bfloat16),
        ),
        in_specs=[vmem, anywhere, anywhere],
        out_specs=(vmem, hbm, hbm),
        scratch_shapes=[pltpu.SemaphoreType.DMA((2,))],
        compiler_params=pltpu.CompilerParams(vmem_limit_bytes=2**20),
        name="hand_over",
    )(*results)
    return loss, image, text


def solution(mesh):
    in_specs = (P(("blk", "inner"), None), P(("blk", "inner"), None), P(), P())
    out_specs = (P(("blk", "inner")), P(("blk", "inner"), None), P(("blk", "inner"), None))
    return jax.shard_map(local, mesh=mesh, in_specs=in_specs, out_specs=out_specs, check_vma=False)
```

```python
import functools
import math
import jax
import jax.numpy as jnp
from jax import lax
from jax.experimental import pallas as pl
from jax.experimental.pallas import tpu as pltpu
from jax.sharding import PartitionSpec as P

MESH = pl.DeviceIdType.MESH
D = 1152
ROWS = 384
SPAN = 4
R = 128
NC = ROWS // R
WIDE = 256
HALF = 640
LOG2E = 1.4426950408889634

P1, P2, P3, Q1, Q2, Q3 = 1, 2, 3, 5, 6, 7
LATE = 8
BOTH = LATE
NOTHING = 0


def packed(*items):
    codes = []
    for begin in range(0, len(items), 6):
        code = 0
        for item in reversed(items[begin : begin + 6]):
            code = code * 16 + item
        codes.append(code)
    return codes


OUTER = packed(Q2, LATE + Q2, Q1, Q3, P1, LATE + Q1, LATE + Q3, LATE + P1, P3, LATE + P3, P2, LATE + P2)
ACROSS = packed(Q2, LATE + Q2, P3, LATE + P3, P1, LATE + P1, Q3, LATE + Q3, Q1, P2, LATE + Q1, LATE + P2)
ALONG = packed(Q2, LATE + Q2, P1, LATE + P1, Q3, LATE + Q3, Q1, P2, P3, LATE + Q1, BOTH, NOTHING)

EARLIEST = 2
FIRST_IN = packed(Q2, LATE + Q2, P1, LATE + P1, P3, LATE + P3, Q1, LATE + Q1, P2, Q3, LATE + Q3, LATE + P2)

ORIGIN = packed(Q2, LATE + Q2, Q3, P1, LATE + Q3, LATE + P1, P3, Q1, LATE + P3, LATE + Q1, P2, LATE + P2)

FOURTH = packed(Q2, LATE + Q2, Q1, P1, LATE + Q1, P3, Q3, LATE + P1, LATE + Q3, LATE + P3, P2, LATE + P2)


def place(index, total):
    index = lax.rem(index + total, total)
    return (lax.div(index, 2), lax.rem(index, 2))


def entries(dots, scale, bias, sign=None):
    power = dots * (scale * LOG2E) + bias * LOG2E
    if sign is not None:
        power = power * sign
    grown = jnp.exp2(power)
    one = 1.0 + grown
    inverse = pl.reciprocal(one, approx=True)
    inverse = inverse * (2.0 - one * inverse)
    term = jnp.where(grown < 0.0078125, grown * (1.0 - grown * (0.5 - grown * (1.0 / 3.0))), jnp.log(one))
    coef = grown * inverse * scale
    if sign is not None:
        coef = coef * sign
    return term, coef.astype(jnp.bfloat16)


def products(near, far, step):
    total = None
    for begin in range(0, D, step):
        width = min(step, D - begin)
        cols = pl.ds(begin, width)
        part = lax.dot_general(
            near[:, cols],
            far[..., cols].reshape(-1, width),
            (((1,), (1,)), ((), ())),
            preferred_element_type=jnp.float32,
        )
        total = part if total is None else total + part
    return total


def lanes(term):
    folded = term[:, :R]
    for j in range(R, term.shape[1], R):
        folded = folded + term[:, j : j + R]
    return folded


def kernel(total, scaling_in, shift_in, picture, caption, loss_out, image_out, text_out,
           raw, buf, grad, loss, inv, in_sem, send_sem, recv_sem, ack):
    blk, inner_index = lax.axis_index("blk"), lax.axis_index("inner")
    me = blk * 2 + inner_index
    core = lax.rem(blk, 2)
    p = core
    q = 1 - core
    sgn = 1 - 2 * core
    outer = 1 - (core - inner_index) * (core - inner_index)

    barrier = pltpu.get_barrier_semaphore()
    for away in (1, 2, 3):
        pl.semaphore_signal(barrier, inc=1, device_id=place(me - away, total), device_id_type=MESH)

    def fetch(kind, c):
        ref = caption if kind == 0 else picture
        rows = pl.ds(c * R, R)
        return pltpu.make_async_copy(ref.at[rows], raw.at[kind, rows], in_sem.at[kind, c])

    for c in range(NC):
        for kind in (0, 1):
            fetch(kind, c).start( )

    def chunk(kind, distance, c):
        start = c * R if isinstance(c, int) else pl.multiple_of(c * R, R)
        return buf.at[kind, distance, pl.ds(start, R)]

    def send(slot, kind, source, target, away, c):
        return pltpu.make_async_remote_copy(
            src_ref=chunk(kind, source, c),
            dst_ref=chunk(kind, target, c),
            send_sem=send_sem.at[slot, c],
            recv_sem=recv_sem.at[kind, target, c],
            device_id=place(me + away, total),
            device_id_type=MESH,
        )

    def s0(c):
        return send(0, p, 0, 1, sgn, c)

    def s1(c):
        return send(1, p, 0, 2, 2 * sgn, c)

    def s2(c):
        return send(2, q, 0, 1, -sgn, c)

    def s3(c):
        return send(3, p, 1, 3, 2 * sgn, c)

    def s4(c):
        return send(4, p, outer, 3 - outer, sgn * (3 - 2 * outer), c)

    def s5(c):
        return send(5, q, outer, 3 - outer, -sgn * (3 - 2 * outer), c)

    def start(*sends):
        for one in sends:
            for c in range(NC):
                one(c).start()

    def normalize(kind, c):
        fetch(kind, c).wait()
        rows = pl.ds(c * R, R)
        values = raw[kind, rows].astype(jnp.float32)
        shrink = 1.0 / jnp.sqrt(jnp.sum(values * values, axis=-1, keepdims=True) + 1e-06)
        inv[kind, rows] = shrink
        buf[kind, 0, rows] = (values * shrink).astype(jnp.bfloat16)

    high = lax.rem(lax.div(blk, 2), 2)
    along = (high - core) * (high - core)
    on_first, on_second = core == 0, core == 1
    is_outer, is_inner = outer == 1, outer == 0

    third_now = is_inner & on_first & (along == 1)
    prompt = me > EARLIEST

    for c in range(NC):
        normalize(0, c)
        if c == 0:
            pl.semaphore_wait(barrier, 3)
            for away in (1, 2, 3):
                pl.semaphore_signal(ack.at[away - 1], inc=1, device_id=place(me + away, total), device_id_type=MESH)

        @pl.when(on_first & is_outer)
        def _():
            s0(c).start()

        @pl.when(on_first & is_inner & (along == 0))
        def _():
            s4(c).start()

        @pl.when(on_second)
        def _():
            s2(c).start()

        normalize(1, c)

        if c == 0:

            @pl.when(prompt)
            def _():
                pl.semaphore_wait(ack.at[0], 1)

            @pl.when(third_now)
            def _():
                pl.semaphore_wait(ack.at[2], 1)

        @pl.when(prompt & on_first)
        def _():
            s2(c).start()

        @pl.when(on_second & is_outer)
        def _():
            s0(c).start()

        @pl.when(third_now)
        def _():
            s5(c).start()

    @pl.when(on_second & is_inner)
    def _():
        start(s5)

    @pl.when(on_first)
    def _():
        start(s1)

    ahead_first = me == EARLIEST - 1

    @pl.when(ahead_first)
    def _():
        start(s0)

    @pl.when(jnp.logical_not(prompt))
    def _():
        pl.semaphore_wait(ack.at[0], 1)

    @pl.when(jnp.logical_not(prompt) & on_first)
    def _():
        start(s2)

    @pl.when(is_inner & jnp.logical_not(ahead_first))
    def _():
        start(s0)

    scale, bias = scaling_in[:1, :1], shift_in[:1, :1]

    row = lax.broadcasted_iota(jnp.int32, (ROWS, ROWS), 0)
    col = lax.broadcasted_iota(jnp.int32, (ROWS, ROWS), 1)
    sign = jnp.where(row == col, jnp.float32(-1.0), jnp.float32(1.0))
    dots = lax.dot_general(buf[1, 0], buf[0, 0], (((1,), (1,)), ((), ())), preferred_element_type=jnp.float32)
    term, coef = entries(dots, scale, bias, sign)
    loss[0] = lanes(term)
    loss[1] = jnp.zeros((ROWS, R), jnp.float32)
    for n in range(0, D, 384):
        cols = pl.ds(n, 384)
        grad[1, :, cols] = jnp.dot(coef, buf[0, 0, :, cols], preferred_element_type=jnp.float32)
        grad[0, :, cols] = lax.dot_general(coef, buf[1, 0, :, cols], (((0,), (0,)), ((), ())), preferred_element_type=jnp.float32)

    pl.semaphore_wait(ack.at[1], 1)

    @pl.when(on_second)
    def _():
        start(s1)

    def late_sends():
        @pl.when(jnp.logical_not(third_now))
        def _():
            pl.semaphore_wait(ack.at[2], 1)

        @pl.when(is_inner & ((along == 1) | on_second))
        def _():
            start(s4)

        @pl.when(is_inner & on_first & (along == 0))
        def _():
            start(s5)

    def arrived(kind, distance, c):
        pltpu.make_async_remote_copy(
            src_ref=chunk(kind, distance, c), dst_ref=chunk(kind, distance, c),
            send_sem=send_sem.at[0, c], recv_sem=recv_sem.at[kind, distance, c],
            device_id=place(me + 1, total), device_id_type=MESH).wait_recv()

    def use(block, first, count):
        second = lax.div(block, 4)
        distance = lax.rem(block, 4)
        kind = p + second * (q - p)
        other = 1 - kind
        for c in range(first, first + count):
            arrived(kind, distance, c)

            @pl.when(block == P1)
            def _():
                s3(c).start()

            @pl.when((block == P1) & is_outer)
            def _():
                s4(c).start()

            @pl.when((block == Q1) & is_outer)
            def _():
                s5(c).start()

        accumulate(kind, buf.at[kind, distance, pl.ds(first * R, count * R)])

    def accumulate(kind, far):
        other = 1 - kind
        rows = math.prod(far.shape) // D
        dots = products(buf.at[other, 0], far, D if rows == WIDE else HALF)
        term, coef = entries(dots, scale, bias)
        loss[kind] += lanes(term)
        for n in range(0, D, 384):
            cols = pl.ds(n, 384)
            grad[other, :, cols] += jnp.dot(
                coef, far[..., cols].reshape(-1, 384), preferred_element_type=jnp.float32
            )

    for half in (0, 1):
        code = outer * OUTER[half] + (1 - outer) * (along * ALONG[half] + (1 - along) * ACROSS[half])
        code = jnp.where(me == EARLIEST, FIRST_IN[half], jnp.where(me == 0, ORIGIN[half], jnp.where(me == 3, FOURTH[half], code)))

        def step(i, code):
            item = lax.rem(code, 16)

            if half == 0:
                pl.when(i == 2)(late_sends)

            @pl.when((item > NOTHING) & (item < LATE))
            def _():
                use(item, 0, WIDE // R)

            if half == 1:

                @pl.when(item == BOTH)
                def _():
                    arrived(p, 2, NC - 1)
                    arrived(p, 3, NC - 1)
                    accumulate(p, buf.at[p, pl.ds(2, 2), pl.ds(WIDE, ROWS - WIDE)])

            @pl.when(item > LATE)
            def _():
                use(item - LATE, WIDE // R, NC - WIDE // R)

            return lax.div(code, 16)

        lax.fori_loop(0, 6, step, code)

    for kind, ref in ((0, text_out), (1, image_out)):
        for r in range(0, ROWS, 32):
            rows = pl.ds(r, 32)
            values = raw[kind, rows].astype(jnp.float32)
            shrink = inv[kind, rows]
            whole = grad[kind, rows]
            along = jnp.sum(values * whole, axis=-1, keepdims=True) * (shrink * shrink)
            ref[rows] = ((whole - values * along) * shrink).astype(jnp.bfloat16)
    loss_out[...] = jnp.sum(loss[0].T, axis=0, keepdims=True) * (1.0 / (SPAN * ROWS))

    for c in range(NC):
        for one in (s0, s1, s2, s3, s4, s5):
            one(c).wait_send()


def hand_over(loss, image, text, loss_out, image_out, text_out, sem):
    copies = [
        pltpu.make_async_copy(source, target, sem.at[i])
        for i, (source, target) in enumerate(((image, image_out), (text, text_out)))
    ]
    for copy in copies:
        copy.start()
    loss_out[...] = loss[0]
    for copy in copies:
        copy.wait()


def local(picture, caption, scaling, shift):
    total = lax.axis_size("blk") * lax.axis_size("inner")
    vmem = pl.BlockSpec(memory_space=pltpu.VMEM)
    hbm = pl.BlockSpec(memory_space=pltpu.HBM)
    picture = pltpu.with_memory_space_constraint(picture, pltpu.HBM)
    caption = pltpu.with_memory_space_constraint(caption, pltpu.HBM)
    results = pl.pallas_call(
        functools.partial(kernel, total),
        out_shape=(
            jax.ShapeDtypeStruct((1, ROWS), jnp.float32),
            jax.ShapeDtypeStruct((ROWS, D), jnp.bfloat16),
            jax.ShapeDtypeStruct((ROWS, D), jnp.bfloat16),
        ),
        in_specs=[vmem, vmem, hbm, hbm],
        out_specs=(vmem, vmem, vmem),
        scratch_shapes=[
            pltpu.VMEM((2, ROWS, D), jnp.bfloat16),
            pltpu.VMEM((2, 4, ROWS, D), jnp.bfloat16),
            pltpu.VMEM((2, ROWS, D), jnp.float32),
            pltpu.VMEM((2, ROWS, R), jnp.float32),
            pltpu.VMEM((2, ROWS, 1), jnp.float32),
            pltpu.SemaphoreType.DMA((2, NC)),
            pltpu.SemaphoreType.DMA((6, NC)),
            pltpu.SemaphoreType.DMA((2, 4, NC)),
            pltpu.SemaphoreType.REGULAR((3,)),
        ],
        compiler_params=pltpu.CompilerParams(collective_id=0, allow_input_fusion=[True, True, False, False], has_side_effects=True, vmem_limit_bytes=40 * 2**20),
    )(jnp.full((8, 128), scaling), jnp.full((8, 128), shift), picture, caption)
    anywhere = pl.BlockSpec(memory_space=pl.ANY)
    loss, image, text = pl.pallas_call(
        hand_over,
        out_shape=(
            jax.ShapeDtypeStruct((ROWS,), jnp.float32),
            jax.ShapeDtypeStruct((ROWS, D), jnp.bfloat16),
            jax.ShapeDtypeStruct((ROWS, D), jnp.bfloat16),
        ),
        in_specs=[vmem, anywhere, anywhere],
        out_specs=(vmem, hbm, hbm),
        scratch_shapes=[pltpu.SemaphoreType.DMA((2,))],
        compiler_params=pltpu.CompilerParams(vmem_limit_bytes=2**20),
        name="hand_over",
    )(*results)
    return loss, image, text


def solution(mesh):
    in_specs = (P(("blk", "inner"), None), P(("blk", "inner"), None), P(), P())
    out_specs = (P(("blk", "inner")), P(("blk", "inner"), None), P(("blk", "inner"), None))
    return jax.shard_map(local, mesh=mesh, in_specs=in_specs, out_specs=out_specs, check_vma=False)
```
